32 devices in a mesh: freq: 2 (over y), rcv: 4 (over z), src: 4 (over x, core).
Axes of the slice: x: 2, y: 2, z: 4, core: 2. Of those that a mesh axis runs over, the one named last changes fastest.
Arguments:
- traces: float32 [256, 2, 4096], P(('freq', 'src'), None, 'rcv'), parts along dimension 0, may hold values from -6 to 6
- moveout: float32 [2, 64, 16], P(None, 'freq'), parts along dimension 1, may hold values from -0.75 to 0.75
- trace_owner: int32 [8192], P(('freq', 'rcv')), parts along dimension 0, may hold values from 0 to 3, as said below
- trace_group: int32 [8192], P(('freq', 'rcv')), parts along dimension 0, may hold values from 0 to 127
- trace_table: int32 [8192], P(('freq', 'rcv')), parts along dimension 0, may hold values from 0 to 31
- aperture: float32 [2, 16384, 8192], P(None, ('freq', 'rcv'), 'src'), parts along dimension 1, may hold values from -0.046875 to 0.046875
- shaping: float32 [256, 2, 8192], P(('freq', 'src'), None, 'rcv'), parts along dimension 0, may hold values from -0.5 to 0.5
Outputs:
- demultiple: float32 [256, 2, 8192], P(('freq', 'src'), None, 'rcv'), parts along dimension 0
The draws below stay inside these ranges and needn't reach their ends.
There are 2 independent parts, one for each index of `freq`. The reference program is written for one: setup_inputs(seed, part) draws one part's arguments, and reference() takes and returns one part's arrays. A program takes and returns all parts, laid end to end along the dimension named above; each array names one. Nothing has to cross between parts.
Inputs may be any that keep to these rules, and one draw needn't show every extreme that they name: `trace_owner`: among the 1024 traces of each index of rcv (aligned blocks of the array), at most 512 name the same owner, and in every draw some owner is named by exactly 512 traces of every block.
All inputs are finite; a program needn't handle non-finite values.
Results may differ from the reference program's by a relative error of at most 0.0001.
Values sent between devices are 32-bit elements; how exact they have to be, the bound alone decides.
No kernel may reach another device: no remote copies, remote signals or barrier semaphores. Data moves between devices by JAX's collectives and lax.ppermute only.
A program may use at most 128 MiB of HBM per device.

```python
import jax
import jax.numpy as jnp
from jax import lax

BINS = 8192
STENCIL = 16
TABLES = 32
ITERS = 2
TRACE_DEV = 1024
SHOTS = 128
TRACES = 4096
GROUPS = 128
CAPACITY = 512
N_RCV = 4


def draw_trace_owner(key, part):
    slot_total = N_RCV * CAPACITY
    owner_of_slot = jnp.arange(slot_total, dtype=jnp.int32) // CAPACITY
    owner_bias = jax.random.randint(jax.random.fold_in(key, 11), (N_RCV,), 0, 4096)
    forced_owner = jax.random.randint(jax.random.fold_in(key, 12), (), 0, N_RCV)

    def one_device(device_index):
        device_key = jax.random.fold_in(jax.random.fold_in(key, 13), device_index)
        slot_noise = jax.random.randint(jax.random.fold_in(device_key, 1), (slot_total,), 0, 4096)
        slot_score = slot_noise + owner_bias[owner_of_slot]
        slot_score = jnp.where(owner_of_slot == forced_owner, -1, slot_score)
        slot_score = (slot_score + 1) * slot_total + jnp.arange(slot_total, dtype=jnp.int32)
        chosen = jnp.argsort(slot_score)[:TRACE_DEV]
        shuffle = jax.random.permutation(jax.random.fold_in(device_key, 2), TRACE_DEV)
        return owner_of_slot[chosen][shuffle]
    return jax.vmap(one_device)(jnp.arange(N_RCV, dtype=jnp.int32)).reshape(-1).astype(jnp.int32)


def place_ends(drawn, own_key, smallest, largest):
    longest = drawn.shape.index(max(drawn.shape))
    spots = []
    for shift in (0, 1):
        where = [jax.random.randint(jax.random.fold_in(own_key, axis), (), 0, length) for axis, length in enumerate(drawn.shape)]
        where[longest] = (where[longest] + shift) % drawn.shape[longest]
        spots.append(tuple(where))
    return drawn.at[spots[0]].set(smallest).at[spots[1]].set(largest)


def block_scale(stream_key, extent, shards, least, largest):
    gain, own = 1.0, jax.random.fold_in(stream_key, 6)
    for dim, blocks in shards:
        heights = jnp.exp(jax.random.uniform(jax.random.fold_in(own, dim), (blocks,), jnp.float32, least / len(shards), largest / len(shards)))
        gain = gain * jnp.repeat(heights, extent[dim] // blocks).reshape([-1 if axis == dim else 1 for axis in range(len(extent))])
    return gain


def gaussian(rng, extent, scale, reach, shards=(), kind=jnp.bfloat16):
    drawn = jax.random.normal(rng, extent, jnp.float32) * scale
    if len(shards) > 0:
        drawn = block_scale(rng, extent, shards, -0.22, 0.18) * drawn
    return jnp.clip(drawn, min=-reach, max=reach).astype(kind)


def setup_inputs(seed: int = 0, part: int = 0) -> dict:
    key_of = jax.random.split(jax.random.key(seed), 8)
    own_keys = jax.random.split(jax.random.fold_in(key_of[7], part), 8)
    return {
        "traces": gaussian(own_keys[0], (SHOTS, 2, TRACES), 1.0, 6.0, ((0, 4), (2, 4)), jnp.float32),
        "moveout": gaussian(own_keys[1], (2, TABLES, STENCIL), 0.125, 0.75, (), jnp.float32),
        "trace_owner": draw_trace_owner(jax.random.fold_in(jax.random.fold_in(key_of[7], part), 71), part),
        "trace_group": place_ends(jax.random.randint(own_keys[3], (TRACES,), 0, GROUPS), jax.random.fold_in(own_keys[3], 1), 0, GROUPS - 1).astype(jnp.int32),
        "trace_table": place_ends(jax.random.randint(own_keys[4], (TRACES,), 0, TABLES), jax.random.fold_in(own_keys[4], 1), 0, TABLES - 1).astype(jnp.int32),
        "aperture": gaussian(own_keys[5], (2, BINS, BINS), (2 * BINS) ** -0.5, 0.046875, ((1, 4), (2, 4)), jnp.float32),
        "shaping": jnp.clip(jax.random.uniform(own_keys[6], (SHOTS, 2, BINS), jnp.float32, -0.5, 0.5) * block_scale(own_keys[6], (SHOTS, 2, BINS), ((0, 4), (2, 4)), -0.4, 0.0), -0.5, 0.5),
    }


def complex_join(partial_terms):
    return jnp.stack([partial_terms[:, 0, 0] - partial_terms[:, 1, 1], partial_terms[:, 0, 1] + partial_terms[:, 1, 0]], axis=1)


def complex_product(left_side, right_side):
    real_part = left_side[:, 0] * right_side[:, 0] - left_side[:, 1] * right_side[:, 1]
    imag_part = left_side[:, 0] * right_side[:, 1] + left_side[:, 1] * right_side[:, 0]
    return jnp.stack([real_part, imag_part], axis=1)


def reference(traces, moveout, trace_owner, trace_group, trace_table, aperture, shaping):
    highest = lax.Precision.HIGHEST
    bin_block = (trace_owner * GROUPS + trace_group).astype(jnp.int32)
    weights = moveout[:, trace_table, :]
    values = jnp.transpose(traces, (2, 1, 0))
    real_part = values[:, 0, None, :] * weights[0][:, :, None] - values[:, 1, None, :] * weights[1][:, :, None]
    real_sum = jax.ops.segment_sum(real_part, bin_block, num_segments=BINS // STENCIL)
    imag_part = values[:, 0, None, :] * weights[1][:, :, None] + values[:, 1, None, :] * weights[0][:, :, None]
    imag_sum = jax.ops.segment_sum(imag_part, bin_block, num_segments=BINS // STENCIL)
    binned = jnp.stack([real_sum, imag_sum], 0).reshape(2, BINS, SHOTS).transpose(2, 0, 1)
    panel_now = binned
    for sweep_index in range(ITERS):
        multiples = complex_join(jnp.einsum("sck,dik->scdi", panel_now, aperture, precision=highest))
        panel_now = binned - complex_product(shaping, multiples)
    return panel_now
```

```python
import functools

import jax
import jax.numpy as jnp
from jax import lax
from jax.experimental import pallas as pl
from jax.experimental.pallas import tpu as pltpu
from jax.sharding import PartitionSpec as P

ITERS = 2
NT = (((1,), (1,)), ((), ()))
NN = (((1,), (0,)), ((), ()))
LANES = 128
VMEM_LIMIT = 56 * 2**20


def split(value):
    high = value.astype(jnp.bfloat16)
    return high, (value - high.astype(jnp.float32)).astype(jnp.bfloat16)


def dot(left, right, dims):
    return lax.dot_general(left, right, dims, preferred_element_type=jnp.float32)


def swap(value, axis, flip):
    size = lax.axis_size(axis)
    return lax.ppermute(value, axis, [(i, i ^ flip) for i in range(size)])


def bits(size):
    return [1 << b for b in range(size.bit_length() - 1)]


def line_gather(value):
    size = lax.axis_size("rcv")
    me = lax.axis_index("rcv")
    got = {0: value}
    for flip in range(1, size, 2):
        got[flip] = swap(value, "rcv", flip)
    for flip in range(2, size, 2):
        near = [abs((i ^ 1) - (i ^ flip)) < abs(i - (i ^ flip)) for i in range(size)]
        direct = lax.ppermute(value, "rcv", [(i ^ flip, i) for i in range(size) if not near[i]])
        relay = lax.ppermute(got[flip ^ 1], "rcv", [(i ^ 1, i) for i in range(size) if near[i]])
        got[flip] = jnp.where(jnp.asarray(near)[me], relay, direct)
    return [got[flip] for flip in range(size)]


def src_gather(value):
    size = lax.axis_size("src")
    got = {0: value}
    for flip in bits(size)[1:] + bits(size)[:1]:
        for key in list(got):
            got[key ^ flip] = swap(got[key], "src", flip)
    return [got[flip] for flip in range(size)]


def src_reduce(pieces):
    size = lax.axis_size("src")
    pieces = dict(enumerate(pieces))
    for flip in bits(size):
        keep = [key for key in pieces if not key & flip]
        pieces = {key: pieces[key] + swap(pieces[key ^ flip], "src", flip) for key in keep}
    return pieces[0]


def bin_kernel(n_group, n_src, first, last, *refs):
    code_ref, matrix_ref, refs = refs[0], refs[1], refs[2:]
    sum_ref, refs = (None, refs) if first else (refs[0], refs[1:])
    piece_refs, (out_ref, high, low) = refs[: n_group * n_src], refs[n_group * n_src :]
    rows, length = piece_refs[0].shape
    step = pl.program_id(0)

    @pl.when(step == 0)
    def _():
        for m in range(n_group):
            for q in range(n_src):
                here = (pl.ds(q * rows, rows), pl.ds(m * length, length))
                high[here], low[here] = split(piece_refs[m * n_src + q][...])

    codes = matrix_ref.shape[1]
    wanted = lax.broadcasted_iota(jnp.int32, (codes, 1), 0) + step * codes
    total = None if first else sum_ref[...]
    for m in range(n_group):
        part = slice(m * length, (m + 1) * length)
        hot = jnp.where(code_ref[m : m + 1, :] == wanted, 1.0, 0.0).astype(jnp.bfloat16)
        term = dot(high[:, part], hot, NT) + dot(low[:, part], hot, NT)
        total = term if total is None else total + term
    if not last:
        out_ref[...] = total
        return
    sum_high, sum_low = split(total)
    both = []
    for d in range(2):
        mat_high, mat_low = split(matrix_ref[d])
        both.append(
            dot(sum_high, mat_high, NN) + dot(sum_high, mat_low, NN) + dot(sum_low, mat_high, NN)
        )
    half = rows // 2
    for q in range(n_src):
        re, im = slice(q * rows, q * rows + half), slice(q * rows + half, (q + 1) * rows)
        out_ref[re, :] = both[0][re] - both[1][im]
        out_ref[im, :] = both[1][re] + both[0][im]


def bin_columns(blocks, codes, moveout, groups):
    n_rcv, n_src = len(blocks), lax.axis_size("src")
    rows, length = blocks[0].shape
    _, tables, stencil = moveout.shape
    per_tile = LANES // stencil
    matrix = jnp.einsum("ab,dkj->dakbj", jnp.eye(per_tile, dtype=jnp.float32), moveout,
                        precision=lax.Precision.HIGHEST)
    matrix = matrix.reshape(2, per_tile * tables, LANES)
    whole = lambda shape: pl.BlockSpec(shape, lambda i: (0,) * len(shape))
    tiled = lambda width: pl.BlockSpec((n_src * rows, width), lambda i: (0, i))
    n_group = min(2, n_rcv)
    sums, done = [], []
    for start in range(0, n_rcv, n_group):
        first, last = start == 0, start + n_group == n_rcv
        group = blocks[start : start + n_group]
        if len(done) >= 2:
            group = lax.optimization_barrier((group, done[-2]))[0]
        flat = [piece for block in group for piece in src_gather(block)]
        here = codes[start : start + n_group]
        width = LANES if last else per_tile * tables
        kernel = functools.partial(bin_kernel, n_group, n_src, first, last)
        total = pl.pallas_call(
            kernel,
            grid=(groups // per_tile,),
            in_specs=[whole(here.shape), whole(matrix.shape)]
            + [tiled(per_tile * tables) for _ in sums]
            + [whole(p.shape) for p in flat],
            out_specs=tiled(width),
            out_shape=jax.ShapeDtypeStruct((n_src * rows, groups // per_tile * width), jnp.float32),
            scratch_shapes=[pltpu.VMEM((n_src * rows, n_group * length), jnp.bfloat16)] * 2,
            compiler_params=pltpu.CompilerParams(vmem_limit_bytes=VMEM_LIMIT),
            name="bin_traces",
        )(here, matrix, *sums, *flat)
        sums = [total]
        done.append(total)
    return sums[0]


def multiply_kernel(n_src, a_ref, x_ref, out_ref, high, low):
    rows = x_ref.shape[0] // n_src
    half = rows // 2

    @pl.when(pl.program_id(0) == 0)
    def _():
        for q in range(n_src):
            re, im = pl.ds(q * rows, half), pl.ds(q * rows + half, half)
            real, imag = x_ref[re, :], x_ref[im, :]
            for d, top, bottom in ((0, real, imag), (1, -imag, real)):
                high[d, re, :], low[d, re, :] = split(top)
                high[d, im, :], low[d, im, :] = split(bottom)

    total = None
    for d in range(2):
        a_high, a_low = split(a_ref[d])
        term = dot(high[d], a_high, NT) + dot(low[d], a_high, NT) + dot(high[d], a_low, NT)
        total = term if total is None else total + term
    out_ref[...] = total


def multiply(columns, aperture):
    n_src = lax.axis_size("src")
    _, out_bins, depth = aperture.shape
    tile = min(512, out_bins)
    return pl.pallas_call(
        lambda *refs: multiply_kernel(n_src, *refs),
        grid=(out_bins // tile,),
        in_specs=[
            pl.BlockSpec((2, tile, depth), lambda i: (0, i, 0)),
            pl.BlockSpec(columns.shape, lambda i: (0, 0)),
        ],
        out_specs=pl.BlockSpec((columns.shape[0], tile), lambda i: (0, i)),
        out_shape=jax.ShapeDtypeStruct((columns.shape[0], out_bins), jnp.float32),
        scratch_shapes=[pltpu.VMEM((2,) + columns.shape, jnp.bfloat16)] * 2,
        compiler_params=pltpu.CompilerParams(vmem_limit_bytes=VMEM_LIMIT),
        name="multiply",
    )(aperture, columns)


def complex_product(left, right):
    return jnp.stack([left[0] * right[0] - left[1] * right[1], left[0] * right[1] + left[1] * right[0]])


def per_device(traces, moveout, trace_owner, trace_group, trace_table, aperture, shaping):
    n_rcv, n_src = lax.axis_size("rcv"), lax.axis_size("src")
    rcv, src = lax.axis_index("rcv"), lax.axis_index("src")
    fold = n_rcv // n_src
    shots, _, length = traces.shape
    _, tables, stencil = moveout.shape
    out_bins = aperture.shape[1]
    groups = out_bins // stencil
    rows = 2 * shots

    values = traces.transpose(1, 0, 2).reshape(rows, length)
    code = ((trace_owner * groups + trace_group) * tables + trace_table).reshape(1, length)
    codes = jnp.concatenate(line_gather(code), axis=0) - src * (fold * groups * tables)
    columns = bin_columns(line_gather(values), codes, moveout, fold * groups)

    pairs = [
        (r * n_src + s, (fold * s + r // n_src) * n_src + r % n_src)
        for r in range(n_rcv)
        for s in range(n_src)
    ]
    own = lax.dynamic_slice(
        columns, (((rcv % n_src) ^ src) * rows, (rcv // n_src) * out_bins), (rows, out_bins)
    )
    binned = lax.ppermute(own, ("rcv", "src"), pairs).reshape(2, shots, out_bins)
    shape_now = shaping.transpose(1, 0, 2)

    for sweep in range(ITERS):
        partial = multiply(columns, aperture)
        mine = src_reduce([partial[q * rows : (q + 1) * rows] for q in range(n_src)])
        panel = binned - complex_product(shape_now, mine.reshape(2, shots, out_bins))
        if sweep == ITERS - 1:
            return panel.transpose(1, 0, 2)
        blocks = jnp.stack(line_gather(panel.reshape(rows, out_bins)))
        parts = []
        for flip in range(n_src):
            for offset in range(fold):
                index = (fold * (src ^ flip) + offset) ^ rcv
                block = lax.dynamic_index_in_dim(blocks, index, 0, keepdims=False)
                parts.append(block if flip == 0 else swap(block, "src", flip))
        columns = jnp.concatenate(
            [jnp.concatenate(parts[q * fold : (q + 1) * fold], axis=1) for q in range(n_src)], axis=0
        )


def solution(mesh):
    in_specs = (
        P(("freq", "src"), None, "rcv"),
        P(None, "freq", None),
        P(("freq", "rcv")),
        P(("freq", "rcv")),
        P(("freq", "rcv")),
        P(None, ("freq", "rcv"), "src"),
        P(("freq", "src"), None, "rcv"),
    )
    out_specs = P(("freq", "src"), None, "rcv")
    return jax.shard_map(
        per_device, mesh=mesh, in_specs=in_specs, out_specs=out_specs, check_vma=False
    )
```

```python
import functools

import jax
import jax.numpy as jnp
from jax import lax
from jax.experimental import pallas as pl
from jax.experimental.pallas import tpu as pltpu
from jax.sharding import PartitionSpec as P

ITERS = 2
NT = (((1,), (1,)), ((), ()))
NN = (((1,), (0,)), ((), ()))
LANES = 128
VMEM_LIMIT = 56 * 2**20


def split(value):
    high = value.astype(jnp.bfloat16)
    return high, (value - high.astype(jnp.float32)).astype(jnp.bfloat16)


def dot(left, right, dims):
    return lax.dot_general(left, right, dims, preferred_element_type=jnp.float32)


def reverse(value, size):
    out, bit = 0, size >> 1
    while bit:
        out, value, bit = out | (bit if value & 1 else 0), value >> 1, bit >> 1
    return out


def turn(value, size):
    count = size.bit_length() - 1
    return sum(((value >> b) & 1) << (count - 1 - b) for b in range(count))


def bits(size):
    return [1 << b for b in range(size.bit_length() - 1)]


def swap(value, axis, flip):
    size = lax.axis_size(axis)
    return lax.ppermute(value, axis, [(i, i ^ flip) for i in range(size)])


def line_step(by_shift, step, *others):
    size = lax.axis_size("rcv")
    up = [(i, i + 1) for i in range(step - 1, size - 1)]
    down = [(i + 1, i) for i in range(size - step)]
    below, above = after((by_shift[1 - step], by_shift[step - 1]), *others)
    by_shift[-step] = lax.ppermute(below, "rcv", up)
    by_shift[step] = lax.ppermute(above, "rcv", down)


def line_block(by_shift, flip):
    size = lax.axis_size("rcv")
    me = lax.axis_index("rcv")
    block = None
    for shift in sorted({(i ^ flip) - i for i in range(size)}):
        here = by_shift[shift]
        block = here if block is None else jnp.where((me ^ flip) - me == shift, here, block)
    return block


def src_gather(value, *others):
    size = lax.axis_size("src")
    got = {0: value}
    for flip in bits(size)[1:] + bits(size)[:1]:
        if flip == 1:
            got = after(got, *others)
        for key in list(got):
            got[key ^ flip] = swap(got[key], "src", flip)
    return [got[flip] for flip in range(size)]


def src_reduce(keep, send, flips):
    size = lax.axis_size("src")
    for flip in flips:
        total = keep + swap(send, "src", flip)
        half = total.shape[0] // 2
        if 2 * flip < size:
            keep, send = total[:half], total[half:]
    return (keep, send) if 2 * flips[-1] < size else total


def after(value, *others):
    return lax.optimization_barrier((value, *others))[0]


def estimate(flops, moved):
    return pl.CostEstimate(flops=int(flops), bytes_accessed=int(moved), transcendentals=0)


def whole(shape):
    return pl.BlockSpec(shape, lambda i: (0,) * len(shape))


def bin_kernel(n_block, n_piece, rows, tile_units, first, last, origin_ref, matrix_ref, *refs):
    sum_ref, refs = (None, refs) if first else (refs[0], refs[1:])
    n_flat = n_block * n_piece
    piece_refs, out_refs, both = refs[:n_flat], refs[n_flat:-1], refs[-1]
    length = piece_refs[0].shape[1]
    all_rows = n_piece * rows
    step = pl.program_id(0)

    @pl.when(step == 0)
    def _():
        for m in range(n_block):
            for q in range(n_piece):
                at, cols = reverse(q, n_piece) * rows, pl.ds(m * length, length)
                high, low = split(piece_refs[m * n_piece + q][:rows, :])
                both[pl.ds(at, rows), cols] = high
                both[pl.ds(all_rows + at, rows), cols] = low

    unit = matrix_ref.shape[0]
    out_refs = out_refs[0]
    wide = unit * tile_units
    total = None if first else sum_ref[...]
    wanted = lax.broadcasted_iota(jnp.int32, (wide, length), 0)
    for m in range(n_block):
        here = piece_refs[m * n_piece][rows : rows + 1, :].astype(jnp.int32)
        here = here - (origin_ref[0] + step * wide)
        hot = jnp.where(here == wanted, 1.0, 0.0).astype(jnp.bfloat16)
        term = dot(both[:, m * length : (m + 1) * length], hot, NT)
        term = term[:all_rows] + term[all_rows:]
        total = term if total is None else total + term
    if not last:
        out_refs[...] = total
        return
    half = rows // 2
    mat_high, mat_low = split(matrix_ref[...])
    for g in range(tile_units):
        sum_high, sum_low = split(total[:, g * unit : (g + 1) * unit])
        product = dot(jnp.concatenate([sum_high, sum_low], axis=0), mat_high, NN)
        product = product[:all_rows] + product[all_rows:] + dot(sum_high, mat_low, NN)
        cols = slice(g * LANES, (g + 1) * LANES)
        for q in range(n_piece):
            re, im = slice(q * rows, q * rows + half), slice(q * rows + half, (q + 1) * rows)
            for here, value in (
                (re, product[re, :LANES] - product[im, LANES:]),
                (im, product[re, LANES:] + product[im, :LANES]),
            ):
                if out_refs.dtype == jnp.float32:
                    out_refs[here, cols] = value
                else:
                    out_refs[0, here, cols], out_refs[1, here, cols] = split(value)


def bin_step(pieces, rows, origin, matrix, units, sums=(), last=True, halves=False):
    n_block, n_piece = len(pieces), len(pieces[0])
    length = pieces[0][0].shape[1]
    all_rows = n_piece * rows
    tile_units = min(4, units)
    tiles = units // tile_units
    width = matrix.shape[0] * tile_units
    lanes = LANES * tile_units
    tiled = lambda size: pl.BlockSpec((all_rows, size), lambda i: (0, i))
    if last and halves:
        out_spec = pl.BlockSpec((2, all_rows, lanes), lambda i: (0, 0, i))
        out_shape = jax.ShapeDtypeStruct((2, all_rows, tiles * lanes), jnp.bfloat16)
    else:
        size = lanes if last else width
        out_spec = tiled(size)
        out_shape = jax.ShapeDtypeStruct((all_rows, tiles * size), jnp.float32)
    flat = [piece for block in pieces for piece in block]
    return pl.pallas_call(
        functools.partial(bin_kernel, n_block, n_piece, rows, tile_units, not sums, last),
        grid=(tiles,),
        in_specs=[pl.BlockSpec(memory_space=pltpu.SMEM), whole(matrix.shape)]
        + [tiled(width) for _ in sums]
        + [whole(p.shape) for p in flat],
        out_specs=[out_spec],
        out_shape=[out_shape],
        scratch_shapes=[pltpu.VMEM((2 * all_rows, n_block * length), jnp.bfloat16)],
        compiler_params=pltpu.CompilerParams(vmem_limit_bytes=VMEM_LIMIT),
        cost_estimate=estimate(
            4 * all_rows * n_block * length * tiles * width, 4 * all_rows * tiles * width
        ),
        name="bin_traces",
    )(jnp.reshape(origin, (1,)).astype(jnp.int32), matrix, *sums, *flat)[0]


def multiply_kernel(n_piece, n_src, n_sum, order_ref, a_ref, *refs):
    x_refs, refs = refs[: max(1, n_piece)], refs[max(1, n_piece) :]
    sum_refs, out_refs = refs[:n_sum], refs[n_sum : n_sum + 2]
    if n_piece:
        both = refs[-1]
        rows, width = x_refs[0].shape

        @pl.when(pl.program_id(0) == 0)
        def _():
            for j in range(n_piece):
                number = reverse(j, n_piece)
                at = (reverse(number % n_src, n_src) ^ order_ref[0]) * rows
                at = pl.ds(pl.multiple_of(at, rows), rows)
                cols = ((number // n_src) ^ order_ref[1]) * width
                cols = pl.ds(pl.multiple_of(cols, width), width)
                both[0, at, cols], both[1, at, cols] = split(x_refs[j][...])
    else:
        both = x_refs[0]
        rows = both.shape[1] // n_src
    all_rows = n_src * rows
    high, stacked = both[0], both[...].reshape(2 * all_rows, both.shape[2])
    products = []
    for d in range(2):
        a_high, a_low = split(a_ref[d])
        wide = dot(stacked, a_high, NT)
        products.append(wide[:all_rows] + wide[all_rows:] + dot(high, a_low, NT))
    half = rows // 2
    for p in range(n_src):
        re, im = slice(p * rows, p * rows + half), slice(p * rows + half, (p + 1) * rows)
        at = p * rows % (all_rows // 2)
        out = p * rows // (all_rows // 2)
        for here, value in (
            (slice(at, at + half), products[0][re] - products[1][im]),
            (slice(at + half, at + rows), products[0][im] + products[1][re]),
        ):
            out_refs[out][here, :] = value if not n_sum else value + sum_refs[out][here, :]


def multiply(columns, order, aperture, depth_part=(0, 1), row_part=(0, 1), sums=(), sums_at=0):
    n_src = lax.axis_size("src")
    _, out_bins, depth = aperture.shape
    pieces = columns if isinstance(columns, list) else []
    depth, out_bins = depth // depth_part[1], out_bins // row_part[1]
    tile = min(512, out_bins)
    first = row_part[0] * (out_bins // tile)
    all_rows = n_src * pieces[0].shape[0] if pieces else columns.shape[1]
    inputs = pieces or [columns]
    out_spec = pl.BlockSpec((all_rows // 2, tile), lambda i: (0, i))
    out_shape = jax.ShapeDtypeStruct((all_rows // 2, out_bins), jnp.float32)
    return pl.pallas_call(
        functools.partial(multiply_kernel, len(pieces), n_src, len(sums)),
        grid=(out_bins // tile,),
        in_specs=[
            pl.BlockSpec(memory_space=pltpu.SMEM),
            pl.BlockSpec((2, tile, depth), lambda i: (0, first + i, depth_part[0])),
        ]
        + [whole(x.shape) for x in inputs]
        + [
            pl.BlockSpec((all_rows // 2, tile), lambda i: (0, sums_at * (out_bins // tile) + i))
            for _ in sums
        ],
        out_specs=[out_spec] * 2,
        out_shape=[out_shape] * 2,
        scratch_shapes=[pltpu.VMEM((2, all_rows, depth), jnp.bfloat16)] if pieces else [],
        compiler_params=pltpu.CompilerParams(vmem_limit_bytes=VMEM_LIMIT),
        cost_estimate=estimate(12 * all_rows * out_bins * depth, 8 * out_bins * depth),
        name="multiply",
    )(order, aperture, *inputs, *sums)


def spread(block, j):
    n_rcv, n_src = lax.axis_size("rcv"), lax.axis_size("src")
    fold = n_rcv // n_src
    pairs = [
        (r * n_src + s, (reverse((r % fold) * n_src + s, n_rcv) ^ j) * n_src + r // fold)
        for r in range(n_rcv)
        for s in range(n_src)
    ]
    return lax.ppermute(block, ("rcv", "src"), pairs)


def complex_product(left, right):
    return jnp.stack([left[0] * right[0] - left[1] * right[1], left[0] * right[1] + left[1] * right[0]])


def per_device(traces, moveout, trace_owner, trace_group, trace_table, aperture, shaping):
    n_rcv, n_src = lax.axis_size("rcv"), lax.axis_size("src")
    rcv, src = lax.axis_index("rcv"), lax.axis_index("src")
    fold = n_rcv // n_src
    shots, _, length = traces.shape
    _, tables, stencil = moveout.shape
    out_bins = aperture.shape[1]
    groups = out_bins // stencil
    rows = 2 * shots
    per_tile = LANES // stencil
    units = groups // per_tile

    parts = 2 if fold == 1 else 1
    quarters = parts
    part_bins = out_bins // parts

    code = ((trace_owner * groups + trace_group) * tables + trace_table).astype(jnp.float32)
    values = traces.transpose(1, 0, 2).reshape(rows, length)
    values = jnp.concatenate([values, jnp.broadcast_to(code, (8, length))], axis=0)
    matrix = jnp.einsum("ab,dkj->akdbj", jnp.eye(per_tile, dtype=jnp.float32), moveout,
                        precision=lax.Precision.HIGHEST)
    matrix = matrix.reshape(per_tile * tables, 2 * LANES)

    by_shift, blocks = {0: values}, [values]
    pieces = src_gather(values)
    origin = src * (fold * groups * tables)
    totals = []
    for m in range(n_rcv):
        if m + 1 < n_rcv:
            line_step(by_shift, m + 1, *totals[m - 2 : m - 1] if m > 1 else ())
            block = line_block(by_shift, m + 1)
            blocks.append(after(block, *totals[m - 1 : m] if m > 0 else ()))
            pieces = after(pieces, blocks[-1])
        last = m == n_rcv - 1
        totals.append(
            bin_step([pieces], rows, origin, matrix, fold * units, tuple(totals[-1:]), last, True)
        )
        if not last:
            pieces = src_gather(blocks[-1], totals[-1])
    columns = totals[-1]
    own = [[block] for block in blocks]
    shape_now = shaping.transpose(1, 0, 2)

    def bin_own(part, *others):
        place = after((rcv * parts + part) * (groups // parts * tables), *others)
        panel = bin_step(own, rows, place, matrix, units // parts)
        return panel.reshape(2, shots, part_bins)

    def subtract(part, mine, of):
        here = slice(part * out_bins // of, (part + 1) * out_bins // of)
        inner = slice((part * parts % of) * part_bins // of, (part * parts % of + parts) * part_bins // of)
        mine = mine.reshape(2, shots, out_bins // of)
        return binned[part * parts // of][:, :, inner] - complex_product(shape_now[:, :, here], mine)

    place = turn(rcv, n_rcv) ^ src
    turned = turn(place % n_src, n_src)
    order = jnp.stack([turned, place // n_src]).astype(jnp.int32)

    flips = bits(n_src)
    near, far = (flips[:1], flips[1:]) if n_src > 2 else ([], flips)
    half = n_rcv // 2
    binned, panels, received = [], [], []
    ready = order
    for h in range(parts):
        keep, send = multiply(columns, ready, aperture, (0, 1), (h, parts))
        if near:
            keep, send = src_reduce(keep, send, near)
        binned.append(bin_own(h, keep, *received[-1] if h else ()))
        if h:
            panel = after(panels[-1], keep)
            received[-1] += [spread(panel, j) for j in range(half, n_rcv)]
        mine = src_reduce(keep, send, far)
        if h:
            mine = after(mine, received[-1])
        panels.append(subtract(h, mine, parts).reshape(rows, part_bins))
        received.append([spread(panels[-1], j) for j in range(half)])
        ready = after(order, panels[-1])

    for sweep in range(1, ITERS):
        sums = []
        for c in range(parts - 1):
            for h in range(parts):
                ready = order
                if c == parts - 2 and h == 1:
                    received[-1] += [spread(after(panels[-1], sums[0]), j) for j in range(half, n_rcv)]
                    ready = after(order, received[-1][:half])
                fill = {"sums": sums[h], "sums_at": 0} if c else {}
                total = multiply(received[c], ready, aperture, (c, parts), (h, parts), **fill)
                sums[h:] = [total]
        if parts == 1:
            received[-1] += [spread(panels[-1], j) for j in range(half, n_rcv)]
        partial = []
        for h in range(quarters):
            fill = {} if parts == 1 else {"sums": sums[h * parts // quarters], "sums_at": h % (quarters // parts)}
            ready = after(order, partial[h - 1]) if h > 0 else order
            keep, send = multiply(received[-1], ready, aperture, (parts - 1, parts), (h, quarters), **fill)
            partial.append(src_reduce(keep, send, near) if near else (keep, send))
        panels = [subtract(h, src_reduce(*partial[h], far), quarters) for h in range(quarters)]
    return jnp.concatenate(panels, axis=2).transpose(1, 0, 2)


def solution(mesh):
    in_specs = (
        P(("freq", "src"), None, "rcv"),
        P(None, "freq", None),
        P(("freq", "rcv")),
        P(("freq", "rcv")),
        P(("freq", "rcv")),
        P(None, ("freq", "rcv"), "src"),
        P(("freq", "src"), None, "rcv"),
    )
    out_specs = P(("freq", "src"), None, "rcv")
    return jax.shard_map(
        per_device, mesh=mesh, in_specs=in_specs, out_specs=out_specs, check_vma=False
    )
```

```python
import functools

import jax
import jax.numpy as jnp
from jax import lax
from jax.experimental import pallas as pl
from jax.experimental.pallas import tpu as pltpu
from jax.sharding import PartitionSpec as P

ITERS = 2
NT = (((1,), (1,)), ((), ()))
NN = (((1,), (0,)), ((), ()))
LANES = 128
VMEM_LIMIT = 56 * 2**20


def split(value):
    high = value.astype(jnp.bfloat16)
    return high, (value - high.astype(jnp.float32)).astype(jnp.bfloat16)


def dot(left, right, dims):
    return lax.dot_general(left, right, dims, preferred_element_type=jnp.float32)


def reverse(value, size):
    out, bit = 0, size >> 1
    while bit:
        out, value, bit = out | (bit if value & 1 else 0), value >> 1, bit >> 1
    return out


def turn(value, size):
    count = size.bit_length() - 1
    return sum(((value >> b) & 1) << (count - 1 - b) for b in range(count))


def bits(size):
    return [1 << b for b in range(size.bit_length() - 1)]


def swap(value, axis, flip):
    size = lax.axis_size(axis)
    return lax.ppermute(value, axis, [(i, i ^ flip) for i in range(size)])


def line_step(by_shift, step, *others):
    size = lax.axis_size("rcv")
    up = [(i, i + 1) for i in range(step - 1, size - 1)]
    down = [(i + 1, i) for i in range(size - step)]
    below, above = after((by_shift[1 - step], by_shift[step - 1]), *others)
    by_shift[-step] = lax.ppermute(below, "rcv", up)
    by_shift[step] = lax.ppermute(above, "rcv", down)


def line_block(by_shift, flip):
    size = lax.axis_size("rcv")
    me = lax.axis_index("rcv")
    block = None
    for shift in sorted({(i ^ flip) - i for i in range(size)}):
        here = by_shift[shift]
        block = here if block is None else jnp.where((me ^ flip) - me == shift, here, block)
    return block


def src_gather(value, *others):
    size = lax.axis_size("src")
    got = {0: value}
    for flip in bits(size)[1:] + bits(size)[:1]:
        if flip == 1:
            got = after(got, *others)
        for key in list(got):
            got[key ^ flip] = swap(got[key], "src", flip)
    return [got[flip] for flip in range(size)]


def src_reduce(keep, send, flips):
    size = lax.axis_size("src")
    for flip in flips:
        total = keep + swap(send, "src", flip)
        half = total.shape[0] // 2
        if 2 * flip < size:
            keep, send = total[:half], total[half:]
    return (keep, send) if 2 * flips[-1] < size else total


def after(value, *others):
    return lax.optimization_barrier((value, *others))[0]


def estimate(flops, moved):
    return pl.CostEstimate(flops=int(flops), bytes_accessed=int(moved), transcendentals=0)


def whole(shape):
    return pl.BlockSpec(shape, lambda i: (0,) * len(shape))


def bin_kernel(n_block, n_piece, rows, tile_units, first, last, origin_ref, matrix_ref, *refs):
    sum_ref, refs = (None, refs) if first else (refs[0], refs[1:])
    n_flat = n_block * n_piece
    piece_refs, out_refs, both = refs[:n_flat], refs[n_flat:-1], refs[-1]
    length = piece_refs[0].shape[1]
    all_rows = n_piece * rows
    step = pl.program_id(0)

    @pl.when(step == 0)
    def _():
        for m in range(n_block):
            for q in range(n_piece):
                at, cols = reverse(q, n_piece) * rows, pl.ds(m * length, length)
                high, low = split(piece_refs[m * n_piece + q][:rows, :])
                both[pl.ds(at, rows), cols] = high
                both[pl.ds(all_rows + at, rows), cols] = low

    unit = matrix_ref.shape[0]
    out_refs = out_refs[0]
    wide = unit * tile_units
    total = None if first else sum_ref[...]
    wanted = lax.broadcasted_iota(jnp.int32, (wide, length), 0)
    for m in range(n_block):
        here = piece_refs[m * n_piece][rows : rows + 1, :].astype(jnp.int32)
        here = here - (origin_ref[0] + step * wide)
        hot = jnp.where(here == wanted, 1.0, 0.0).astype(jnp.bfloat16)
        term = dot(both[:, m * length : (m + 1) * length], hot, NT)
        term = term[:all_rows] + term[all_rows:]
        total = term if total is None else total + term
    if not last:
        out_refs[...] = total
        return
    half = rows // 2
    mat_high, mat_low = split(matrix_ref[...])
    for g in range(tile_units):
        sum_high, sum_low = split(total[:, g * unit : (g + 1) * unit])
        product = dot(jnp.concatenate([sum_high, sum_low], axis=0), mat_high, NN)
        product = product[:all_rows] + product[all_rows:] + dot(sum_high, mat_low, NN)
        cols = slice(g * LANES, (g + 1) * LANES)
        for q in range(n_piece):
            re, im = slice(q * rows, q * rows + half), slice(q * rows + half, (q + 1) * rows)
            for here, value in (
                (re, product[re, :LANES] - product[im, LANES:]),
                (im, product[re, LANES:] + product[im, :LANES]),
            ):
                if out_refs.dtype == jnp.float32:
                    out_refs[here, cols] = value
                else:
                    out_refs[0, here, cols], out_refs[1, here, cols] = split(value)


def bin_step(pieces, rows, origin, matrix, units, sums=(), last=True, halves=False):
    n_block, n_piece = len(pieces), len(pieces[0])
    length = pieces[0][0].shape[1]
    all_rows = n_piece * rows
    tile_units = min(4, units)
    tiles = units // tile_units
    width = matrix.shape[0] * tile_units
    lanes = LANES * tile_units
    tiled = lambda size: pl.BlockSpec((all_rows, size), lambda i: (0, i))
    if last and halves:
        out_spec = pl.BlockSpec((2, all_rows, lanes), lambda i: (0, 0, i))
        out_shape = jax.ShapeDtypeStruct((2, all_rows, tiles * lanes), jnp.bfloat16)
    else:
        size = lanes if last else width
        out_spec = tiled(size)
        out_shape = jax.ShapeDtypeStruct((all_rows, tiles * size), jnp.float32)
    flat = [piece for block in pieces for piece in block]
    return pl.pallas_call(
        functools.partial(bin_kernel, n_block, n_piece, rows, tile_units, not sums, last),
        grid=(tiles,),
        in_specs=[pl.BlockSpec(memory_space=pltpu.SMEM), whole(matrix.shape)]
        + [tiled(width) for _ in sums]
        + [whole(p.shape) for p in flat],
        out_specs=[out_spec],
        out_shape=[out_shape],
        scratch_shapes=[pltpu.VMEM((2 * all_rows, n_block * length), jnp.bfloat16)],
        compiler_params=pltpu.CompilerParams(vmem_limit_bytes=VMEM_LIMIT),
        cost_estimate=estimate(
            4 * all_rows * n_block * length * tiles * width, 4 * all_rows * tiles * width
        ),
        name="bin_traces",
    )(jnp.reshape(origin, (1,)).astype(jnp.int32), matrix, *sums, *flat)[0]


def multiply_kernel(n_piece, n_src, n_sum, order_ref, a_ref, *refs):
    x_refs, refs = refs[: max(1, n_piece)], refs[max(1, n_piece) :]
    sum_refs, out_refs = refs[:n_sum], refs[n_sum : n_sum + 2]
    if n_piece:
        both = refs[-1]
        rows, width = x_refs[0].shape

        @pl.when(pl.program_id(0) == 0)
        def _():
            for j in range(n_piece):
                number = reverse(j, n_piece)
                at = (reverse(number % n_src, n_src) ^ order_ref[0]) * rows
                at = pl.ds(pl.multiple_of(at, rows), rows)
                cols = ((number // n_src) ^ order_ref[1]) * width
                cols = pl.ds(pl.multiple_of(cols, width), width)
                both[0, at, cols], both[1, at, cols] = split(x_refs[j][...])
    else:
        both = x_refs[0]
        rows = both.shape[1] // n_src
    all_rows = n_src * rows
    high, stacked = both[0], both[...].reshape(2 * all_rows, both.shape[2])
    products = []
    for d in range(2):
        a_high, a_low = split(a_ref[d])
        wide = dot(stacked, a_high, NT)
        products.append(wide[:all_rows] + wide[all_rows:] + dot(high, a_low, NT))
    half = rows // 2
    for p in range(n_src):
        re, im = slice(p * rows, p * rows + half), slice(p * rows + half, (p + 1) * rows)
        at = p * rows % (all_rows // 2)
        out = p * rows // (all_rows // 2)
        for here, value in (
            (slice(at, at + half), products[0][re] - products[1][im]),
            (slice(at + half, at + rows), products[0][im] + products[1][re]),
        ):
            out_refs[out][here, :] = value if not n_sum else value + sum_refs[out][here, :]


def multiply(columns, order, aperture, depth_part=(0, 1), row_part=(0, 1), sums=(), sums_at=0):
    n_src = lax.axis_size("src")
    _, out_bins, depth = aperture.shape
    pieces = columns if isinstance(columns, list) else []
    depth, out_bins = depth // depth_part[1], out_bins // row_part[1]
    tile = min(512, out_bins)
    first = row_part[0] * (out_bins // tile)
    all_rows = n_src * pieces[0].shape[0] if pieces else columns.shape[1]
    inputs = pieces or [columns]
    out_spec = pl.BlockSpec((all_rows // 2, tile), lambda i: (0, i))
    out_shape = jax.ShapeDtypeStruct((all_rows // 2, out_bins), jnp.float32)
    return pl.pallas_call(
        functools.partial(multiply_kernel, len(pieces), n_src, len(sums)),
        grid=(out_bins // tile,),
        in_specs=[
            pl.BlockSpec(memory_space=pltpu.SMEM),
            pl.BlockSpec((2, tile, depth), lambda i: (0, first + i, depth_part[0])),
        ]
        + [whole(x.shape) for x in inputs]
        + [
            pl.BlockSpec((all_rows // 2, tile), lambda i: (0, sums_at * (out_bins // tile) + i))
            for _ in sums
        ],
        out_specs=[out_spec] * 2,
        out_shape=[out_shape] * 2,
        scratch_shapes=[pltpu.VMEM((2, all_rows, depth), jnp.bfloat16)] if pieces else [],
        compiler_params=pltpu.CompilerParams(vmem_limit_bytes=VMEM_LIMIT),
        cost_estimate=estimate(12 * all_rows * out_bins * depth, 8 * out_bins * depth),
        name="multiply",
    )(order, aperture, *inputs, *sums)


def spread(block, j):
    n_rcv, n_src = lax.axis_size("rcv"), lax.axis_size("src")
    fold = n_rcv // n_src
    pairs = [
        (r * n_src + s, (reverse((r % fold) * n_src + s, n_rcv) ^ j) * n_src + r // fold)
        for r in range(n_rcv)
        for s in range(n_src)
    ]
    return lax.ppermute(block, ("rcv", "src"), pairs)


def complex_product(left, right):
    return jnp.stack([left[0] * right[0] - left[1] * right[1], left[0] * right[1] + left[1] * right[0]])


def per_device(traces, moveout, trace_owner, trace_group, trace_table, aperture, shaping):
    n_rcv, n_src = lax.axis_size("rcv"), lax.axis_size("src")
    rcv, src = lax.axis_index("rcv"), lax.axis_index("src")
    fold = n_rcv // n_src
    shots, _, length = traces.shape
    _, tables, stencil = moveout.shape
    out_bins = aperture.shape[1]
    groups = out_bins // stencil
    rows = 2 * shots
    per_tile = LANES // stencil
    units = groups // per_tile

    parts = 1
    quarters = parts
    part_bins = out_bins // parts

    code = ((trace_owner * groups + trace_group) * tables + trace_table).astype(jnp.float32)
    values = traces.transpose(1, 0, 2).reshape(rows, length)
    values = jnp.concatenate([values, jnp.broadcast_to(code, (8, length))], axis=0)
    matrix = jnp.einsum("ab,dkj->akdbj", jnp.eye(per_tile, dtype=jnp.float32), moveout,
                        precision=lax.Precision.HIGHEST)
    matrix = matrix.reshape(per_tile * tables, 2 * LANES)

    by_shift, blocks = {0: values}, [values]
    pieces = src_gather(values)
    origin = src * (fold * groups * tables)
    totals = []
    for m in range(n_rcv):
        if m + 1 < n_rcv:
            line_step(by_shift, m + 1, *totals[m - 2 : m - 1] if m > 1 else ())
            block = line_block(by_shift, m + 1)
            blocks.append(after(block, *totals[m - 1 : m] if m > 0 else ()))
            pieces = after(pieces, blocks[-1])
        last = m == n_rcv - 1
        totals.append(
            bin_step([pieces], rows, origin, matrix, fold * units, tuple(totals[-1:]), last, True)
        )
        if not last:
            pieces = src_gather(blocks[-1], totals[-1])
    columns = totals[-1]
    own = [[block] for block in blocks]
    shape_now = shaping.transpose(1, 0, 2)

    def bin_own(part, *others):
        place = after((rcv * parts + part) * (groups // parts * tables), *others)
        panel = bin_step(own, rows, place, matrix, units // parts)
        return panel.reshape(2, shots, part_bins)

    def subtract(part, mine, of):
        here = slice(part * out_bins // of, (part + 1) * out_bins // of)
        inner = slice((part * parts % of) * part_bins // of, (part * parts % of + parts) * part_bins // of)
        mine = mine.reshape(2, shots, out_bins // of)
        return binned[part * parts // of][:, :, inner] - complex_product(shape_now[:, :, here], mine)

    place = turn(rcv, n_rcv) ^ src
    turned = turn(place % n_src, n_src)
    order = jnp.stack([turned, place // n_src]).astype(jnp.int32)

    flips = bits(n_src)
    near, far = (flips[:1], flips[1:]) if n_src > 2 else ([], flips)
    half = n_rcv // 2
    binned, panels, received = [], [], []
    ready = order
    for h in range(parts):
        keep, send = multiply(columns, ready, aperture, (0, 1), (h, parts))
        if near:
            keep, send = src_reduce(keep, send, near)
        binned.append(bin_own(h, keep, *received[-1] if h else ()))
        if h:
            panel = after(panels[-1], keep)
            received[-1] += [spread(panel, j) for j in range(half, n_rcv)]
        mine = src_reduce(keep, send, far)
        if h:
            mine = after(mine, received[-1])
        panels.append(subtract(h, mine, parts).reshape(rows, part_bins))
        received.append([spread(panels[-1], j) for j in range(half)])
        ready = after(order, panels[-1])

    for sweep in range(1, ITERS):
        sums = []
        for c in range(parts - 1):
            for h in range(parts):
                ready = order
                if c == parts - 2 and h == 1:
                    received[-1] += [spread(after(panels[-1], sums[0]), j) for j in range(half, n_rcv)]
                    ready = after(order, received[-1][:half])
                fill = {"sums": sums[h], "sums_at": 0} if c else {}
                total = multiply(received[c], ready, aperture, (c, parts), (h, parts), **fill)
                sums[h:] = [total]
        if parts == 1:
            received[-1] += [spread(panels[-1], j) for j in range(half, n_rcv)]
        partial = []
        for h in range(quarters):
            fill = {} if parts == 1 else {"sums": sums[h * parts // quarters], "sums_at": h % (quarters // parts)}
            ready = after(order, partial[h - 1]) if h > 0 else order
            keep, send = multiply(received[-1], ready, aperture, (parts - 1, parts), (h, quarters), **fill)
            partial.append(src_reduce(keep, send, near) if near else (keep, send))
        panels = [subtract(h, src_reduce(*partial[h], far), quarters) for h in range(quarters)]
    return jnp.concatenate(panels, axis=2).transpose(1, 0, 2)


def solution(mesh):
    in_specs = (
        P(("freq", "src"), None, "rcv"),
        P(None, "freq", None),
        P(("freq", "rcv")),
        P(("freq", "rcv")),
        P(("freq", "rcv")),
        P(None, ("freq", "rcv"), "src"),
        P(("freq", "src"), None, "rcv"),
    )
    out_specs = P(("freq", "src"), None, "rcv")
    return jax.shard_map(
        per_device, mesh=mesh, in_specs=in_specs, out_specs=out_specs, check_vma=False
    )
```

```python
import functools

import jax
import jax.numpy as jnp
from jax import lax
from jax.experimental import pallas as pl
from jax.experimental.pallas import tpu as pltpu
from jax.sharding import PartitionSpec as P

ITERS = 2
NT = (((1,), (1,)), ((), ()))
NN = (((1,), (0,)), ((), ()))
LANES = 128
VMEM_LIMIT = 56 * 2**20


def split(value):
    high = value.astype(jnp.bfloat16)
    return high, (value - high.astype(jnp.float32)).astype(jnp.bfloat16)


def dot(left, right, dims):
    return lax.dot_general(left, right, dims, preferred_element_type=jnp.float32)


def reverse(value, size):
    out, bit = 0, size >> 1
    while bit:
        out, value, bit = out | (bit if value & 1 else 0), value >> 1, bit >> 1
    return out


def turn(value, size):
    count = size.bit_length() - 1
    return sum(((value >> b) & 1) << (count - 1 - b) for b in range(count))


def bits(size):
    return [1 << b for b in range(size.bit_length() - 1)]


def swap(value, axis, flip):
    size = lax.axis_size(axis)
    return lax.ppermute(value, axis, [(i, i ^ flip) for i in range(size)])


def line_step(by_shift, step, *others):
    size = lax.axis_size("rcv")
    up = [(i, i + 1) for i in range(step - 1, size - 1)]
    down = [(i + 1, i) for i in range(size - step)]
    below, above = after((by_shift[1 - step], by_shift[step - 1]), *others)
    by_shift[-step] = lax.ppermute(below, "rcv", up)
    by_shift[step] = lax.ppermute(above, "rcv", down)


def line_block(by_shift, flip):
    size = lax.axis_size("rcv")
    me = lax.axis_index("rcv")
    block = None
    for shift in sorted({(i ^ flip) - i for i in range(size)}):
        here = by_shift[shift]
        block = here if block is None else jnp.where((me ^ flip) - me == shift, here, block)
    return block


def src_gather(value, *others):
    size = lax.axis_size("src")
    got = {0: value}
    for flip in bits(size)[1:] + bits(size)[:1]:
        if flip == 1:
            got = after(got, *others)
        for key in list(got):
            got[key ^ flip] = swap(got[key], "src", flip)
    return [got[flip] for flip in range(size)]


def src_reduce(keep, send, flips):
    size = lax.axis_size("src")
    for flip in flips:
        total = keep + swap(send, "src", flip)
        half = total.shape[0] // 2
        if 2 * flip < size:
            keep, send = total[:half], total[half:]
    return (keep, send) if 2 * flips[-1] < size else total


def after(value, *others):
    return lax.optimization_barrier((value, *others))[0]


def estimate(flops, moved):
    return pl.CostEstimate(flops=int(flops), bytes_accessed=int(moved), transcendentals=0)


def whole(shape):
    return pl.BlockSpec(shape, lambda i: (0,) * len(shape))


def bin_kernel(n_block, n_piece, rows, tile_units, first, last, origin_ref, matrix_ref, *refs):
    sum_ref, refs = (None, refs) if first else (refs[0], refs[1:])
    n_flat = n_block * n_piece
    piece_refs, out_refs, both = refs[:n_flat], refs[n_flat:-1], refs[-1]
    length = piece_refs[0].shape[1]
    all_rows = n_piece * rows
    step = pl.program_id(0)

    @pl.when(step == 0)
    def _():
        for m in range(n_block):
            for q in range(n_piece):
                at, cols = reverse(q, n_piece) * rows, pl.ds(m * length, length)
                high, low = split(piece_refs[m * n_piece + q][:rows, :])
                both[pl.ds(at, rows), cols] = high
                both[pl.ds(all_rows + at, rows), cols] = low

    unit = matrix_ref.shape[0]
    out_refs = out_refs[0]
    wide = unit * tile_units
    total = None if first else sum_ref[...]
    wanted = lax.broadcasted_iota(jnp.int32, (wide, length), 0)
    for m in range(n_block):
        here = piece_refs[m * n_piece][rows : rows + 1, :].astype(jnp.int32)
        here = here - (origin_ref[0] + step * wide)
        hot = jnp.where(here == wanted, 1.0, 0.0).astype(jnp.bfloat16)
        term = dot(both[:, m * length : (m + 1) * length], hot, NT)
        term = term[:all_rows] + term[all_rows:]
        total = term if total is None else total + term
    if not last:
        out_refs[...] = total
        return
    half = rows // 2
    mat_high, mat_low = split(matrix_ref[...])
    for g in range(tile_units):
        sum_high, sum_low = split(total[:, g * unit : (g + 1) * unit])
        product = dot(jnp.concatenate([sum_high, sum_low], axis=0), mat_high, NN)
        product = product[:all_rows] + product[all_rows:] + dot(sum_high, mat_low, NN)
        cols = slice(g * LANES, (g + 1) * LANES)
        for q in range(n_piece):
            re, im = slice(q * rows, q * rows + half), slice(q * rows + half, (q + 1) * rows)
            for here, value in (
                (re, product[re, :LANES] - product[im, LANES:]),
                (im, product[re, LANES:] + product[im, :LANES]),
            ):
                if out_refs.dtype == jnp.float32:
                    out_refs[here, cols] = value
                else:
                    out_refs[0, here, cols], out_refs[1, here, cols] = split(value)


def bin_step(pieces, rows, origin, matrix, units, sums=(), last=True, halves=False):
    n_block, n_piece = len(pieces), len(pieces[0])
    length = pieces[0][0].shape[1]
    all_rows = n_piece * rows
    tile_units = min(8, units)
    tiles = units // tile_units
    width = matrix.shape[0] * tile_units
    lanes = LANES * tile_units
    tiled = lambda size: pl.BlockSpec((all_rows, size), lambda i: (0, i))
    if last and halves:
        out_spec = pl.BlockSpec((2, all_rows, lanes), lambda i: (0, 0, i))
        out_shape = jax.ShapeDtypeStruct((2, all_rows, tiles * lanes), jnp.bfloat16)
    else:
        size = lanes if last else width
        out_spec = tiled(size)
        out_shape = jax.ShapeDtypeStruct((all_rows, tiles * size), jnp.float32)
    flat = [piece for block in pieces for piece in block]
    return pl.pallas_call(
        functools.partial(bin_kernel, n_block, n_piece, rows, tile_units, not sums, last),
        grid=(tiles,),
        in_specs=[pl.BlockSpec(memory_space=pltpu.SMEM), whole(matrix.shape)]
        + [tiled(width) for _ in sums]
        + [whole(p.shape) for p in flat],
        out_specs=[out_spec],
        out_shape=[out_shape],
        scratch_shapes=[pltpu.VMEM((2 * all_rows, n_block * length), jnp.bfloat16)],
        compiler_params=pltpu.CompilerParams(vmem_limit_bytes=VMEM_LIMIT),
        cost_estimate=estimate(
            4 * all_rows * n_block * length * tiles * width, 4 * all_rows * tiles * width
        ),
        name="bin_traces",
    )(jnp.reshape(origin, (1,)).astype(jnp.int32), matrix, *sums, *flat)[0]


def multiply_kernel(n_piece, n_src, n_sum, order_ref, a_ref, *refs):
    x_refs, refs = refs[: max(1, n_piece)], refs[max(1, n_piece) :]
    sum_refs, out_refs = refs[:n_sum], refs[n_sum : n_sum + 2]
    if n_piece:
        both = refs[-1]
        rows, width = x_refs[0].shape

        @pl.when(pl.program_id(0) == 0)
        def _():
            for j in range(n_piece):
                number = reverse(j, n_piece)
                at = (reverse(number % n_src, n_src) ^ order_ref[0]) * rows
                at = pl.ds(pl.multiple_of(at, rows), rows)
                cols = ((number // n_src) ^ order_ref[1]) * width
                cols = pl.ds(pl.multiple_of(cols, width), width)
                both[0, at, cols], both[1, at, cols] = split(x_refs[j][...])
    else:
        both = x_refs[0]
        rows = both.shape[1] // n_src
    all_rows = n_src * rows
    high, stacked = both[0], both[...].reshape(2 * all_rows, both.shape[2])
    products = []
    for d in range(2):
        a_high, a_low = split(a_ref[d])
        wide = dot(stacked, a_high, NT)
        products.append(wide[:all_rows] + wide[all_rows:] + dot(high, a_low, NT))
    half = rows // 2
    for p in range(n_src):
        re, im = slice(p * rows, p * rows + half), slice(p * rows + half, (p + 1) * rows)
        at = p * rows % (all_rows // 2)
        out = p * rows // (all_rows // 2)
        for here, value in (
            (slice(at, at + half), products[0][re] - products[1][im]),
            (slice(at + half, at + rows), products[0][im] + products[1][re]),
        ):
            out_refs[out][here, :] = value if not n_sum else value + sum_refs[out][here, :]


def multiply(columns, order, aperture, depth_part=(0, 1), row_part=(0, 1), sums=(), sums_at=0):
    n_src = lax.axis_size("src")
    _, out_bins, depth = aperture.shape
    pieces = columns if isinstance(columns, list) else []
    depth, out_bins = depth // depth_part[1], out_bins // row_part[1]
    tile = min(512, out_bins)
    first = row_part[0] * (out_bins // tile)
    all_rows = n_src * pieces[0].shape[0] if pieces else columns.shape[1]
    inputs = pieces or [columns]
    out_spec = pl.BlockSpec((all_rows // 2, tile), lambda i: (0, i))
    out_shape = jax.ShapeDtypeStruct((all_rows // 2, out_bins), jnp.float32)
    return pl.pallas_call(
        functools.partial(multiply_kernel, len(pieces), n_src, len(sums)),
        grid=(out_bins // tile,),
        in_specs=[
            pl.BlockSpec(memory_space=pltpu.SMEM),
            pl.BlockSpec((2, tile, depth), lambda i: (0, first + i, depth_part[0])),
        ]
        + [whole(x.shape) for x in inputs]
        + [
            pl.BlockSpec((all_rows // 2, tile), lambda i: (0, sums_at * (out_bins // tile) + i))
            for _ in sums
        ],
        out_specs=[out_spec] * 2,
        out_shape=[out_shape] * 2,
        scratch_shapes=[pltpu.VMEM((2, all_rows, depth), jnp.bfloat16)] if pieces else [],
        compiler_params=pltpu.CompilerParams(vmem_limit_bytes=VMEM_LIMIT),
        cost_estimate=estimate(12 * all_rows * out_bins * depth, 8 * out_bins * depth),
        name="multiply",
    )(order, aperture, *inputs, *sums)


def spread(block, j):
    n_rcv, n_src = lax.axis_size("rcv"), lax.axis_size("src")
    fold = n_rcv // n_src
    pairs = [
        (r * n_src + s, (reverse((r % fold) * n_src + s, n_rcv) ^ j) * n_src + r // fold)
        for r in range(n_rcv)
        for s in range(n_src)
    ]
    return lax.ppermute(block, ("rcv", "src"), pairs)


def complex_product(left, right):
    return jnp.stack([left[0] * right[0] - left[1] * right[1], left[0] * right[1] + left[1] * right[0]])


def per_device(traces, moveout, trace_owner, trace_group, trace_table, aperture, shaping):
    n_rcv, n_src = lax.axis_size("rcv"), lax.axis_size("src")
    rcv, src = lax.axis_index("rcv"), lax.axis_index("src")
    fold = n_rcv // n_src
    shots, _, length = traces.shape
    _, tables, stencil = moveout.shape
    out_bins = aperture.shape[1]
    groups = out_bins // stencil
    rows = 2 * shots
    per_tile = LANES // stencil
    units = groups // per_tile

    parts = 1
    quarters = parts
    part_bins = out_bins // parts

    code = ((trace_owner * groups + trace_group) * tables + trace_table).astype(jnp.float32)
    values = traces.transpose(1, 0, 2).reshape(rows, length)
    values = jnp.concatenate([values, jnp.broadcast_to(code, (8, length))], axis=0)
    matrix = jnp.einsum("ab,dkj->akdbj", jnp.eye(per_tile, dtype=jnp.float32), moveout,
                        precision=lax.Precision.HIGHEST)
    matrix = matrix.reshape(per_tile * tables, 2 * LANES)

    by_shift, blocks = {0: values}, [values]
    pieces = src_gather(values)
    origin = src * (fold * groups * tables)
    totals = []
    for m in range(n_rcv):
        if m + 1 < n_rcv:
            line_step(by_shift, m + 1, *totals[m - 2 : m - 1] if m > 1 else ())
            block = line_block(by_shift, m + 1)
            blocks.append(after(block, *totals[m - 1 : m] if m > 0 else ()))
            pieces = after(pieces, blocks[-1])
        last = m == n_rcv - 1
        totals.append(
            bin_step([pieces], rows, origin, matrix, fold * units, tuple(totals[-1:]), last, True)
        )
        if not last:
            pieces = src_gather(blocks[-1], totals[-1])
    columns = totals[-1]
    own = [[block] for block in blocks]
    shape_now = shaping.transpose(1, 0, 2)

    def bin_own(part, *others):
        place = after((rcv * parts + part) * (groups // parts * tables), *others)
        panel = bin_step(own, rows, place, matrix, units // parts)
        return panel.reshape(2, shots, part_bins)

    def subtract(part, mine, of):
        here = slice(part * out_bins // of, (part + 1) * out_bins // of)
        inner = slice((part * parts % of) * part_bins // of, (part * parts % of + parts) * part_bins // of)
        mine = mine.reshape(2, shots, out_bins // of)
        return binned[part * parts // of][:, :, inner] - complex_product(shape_now[:, :, here], mine)

    place = turn(rcv, n_rcv) ^ src
    turned = turn(place % n_src, n_src)
    order = jnp.stack([turned, place // n_src]).astype(jnp.int32)

    flips = bits(n_src)
    near, far = (flips[:1], flips[1:]) if n_src > 2 else ([], flips)
    half = n_rcv // 2
    binned, panels, received = [], [], []
    ready = order
    for h in range(parts):
        keep, send = multiply(columns, ready, aperture, (0, 1), (h, parts))
        if near:
            keep, send = src_reduce(keep, send, near)
        binned.append(bin_own(h, keep, *received[-1] if h else ()))
        if h:
            panel = after(panels[-1], keep)
            received[-1] += [spread(panel, j) for j in range(half, n_rcv)]
        mine = src_reduce(keep, send, far)
        if h:
            mine = after(mine, received[-1])
        panels.append(subtract(h, mine, parts).reshape(rows, part_bins))
        received.append([spread(panels[-1], j) for j in range(half)])
        ready = after(order, panels[-1])

    for sweep in range(1, ITERS):
        sums = []
        for c in range(parts - 1):
            for h in range(parts):
                ready = order
                if c == parts - 2 and h == 1:
                    received[-1] += [spread(after(panels[-1], sums[0]), j) for j in range(half, n_rcv)]
                    ready = after(order, received[-1][:half])
                fill = {"sums": sums[h], "sums_at": 0} if c else {}
                total = multiply(received[c], ready, aperture, (c, parts), (h, parts), **fill)
                sums[h:] = [total]
        if parts == 1:
            received[-1] += [spread(panels[-1], j) for j in range(half, n_rcv)]
        partial = []
        for h in range(quarters):
            fill = {} if parts == 1 else {"sums": sums[h * parts // quarters], "sums_at": h % (quarters // parts)}
            ready = after(order, partial[h - 1]) if h > 0 else order
            keep, send = multiply(received[-1], ready, aperture, (parts - 1, parts), (h, quarters), **fill)
            partial.append(src_reduce(keep, send, near) if near else (keep, send))
        panels = [subtract(h, src_reduce(*partial[h], far), quarters) for h in range(quarters)]
    return jnp.concatenate(panels, axis=2).transpose(1, 0, 2)


def solution(mesh):
    in_specs = (
        P(("freq", "src"), None, "rcv"),
        P(None, "freq", None),
        P(("freq", "rcv")),
        P(("freq", "rcv")),
        P(("freq", "rcv")),
        P(None, ("freq", "rcv"), "src"),
        P(("freq", "src"), None, "rcv"),
    )
    out_specs = P(("freq", "src"), None, "rcv")
    return jax.shard_map(
        per_device, mesh=mesh, in_specs=in_specs, out_specs=out_specs, check_vma=False
    )
```
